32 devices in a mesh: groups: 2 (over y), batch: 4 (over z), tensor: 4 (over x, core).
Axes of the slice: x: 2, y: 2, z: 4, core: 2. Of those that a mesh axis runs over, the one named last changes fastest.
Arguments:
- hidden: bfloat16 [8, 8192], P(('groups', 'batch')), parts along dimension 0, may hold values from -6 to 6
- self_norm: bfloat16 [8192], replicated, may hold values from 0.5 to 1.5
- self_query: bfloat16 [8192, 8192], P('batch', 'tensor'), may hold values from -0.0625 to 0.0625
- self_keyval: bfloat16 [8192, 2048], P('batch', 'tensor'), may hold values from -0.0625 to 0.0625
- self_output: bfloat16 [8192, 8192], P('tensor', 'batch'), may hold values from -0.0625 to 0.0625
- key_cache: bfloat16 [8, 1024, 2048], P(('groups', 'batch'), None, 'tensor'), parts along dimension 0, may hold values from -6 to 6
- cache_lengths: int32 [8], P(('groups', 'batch')), parts along dimension 0, may hold values from 1 to 1024, as said below
- cross_norm: bfloat16 [8192], replicated, may hold values from 0.5 to 1.5
- cross_query: bfloat16 [8192, 8192], P('batch', 'tensor'), may hold values from -0.0625 to 0.0625
- query_gain: float32 [128], replicated, may hold values from 0.5 to 2
- key_gain: float32 [128], replicated, may hold values from 0.5 to 2
- cross_output: bfloat16 [8192, 8192], P('tensor', 'batch'), may hold values from -0.0625 to 0.0625
- cross_gate: float32 [1], replicated, may hold values from 0.3 to 1.2
- image_keyval: bfloat16 [32, 320, 2048], P(('groups', 'batch'), None, 'tensor'), parts along dimension 0, may hold values from -6 to 6
- tile_count: int32 [8], P('groups'), parts along dimension 0, may hold values from 1 to 4
- tile_place: int32 [8, 4], P('groups'), parts along dimension 0, may hold values from 0 to 15, as said below
Outputs:
- layer_output: bfloat16 [8, 8192], P(('groups', 'batch')), parts along dimension 0
The draws below stay inside these ranges and needn't reach their ends.
There are 2 independent parts, one for each index of `groups`. The reference program is written for one: setup_inputs(seed, part) draws one part's arguments, and reference() takes and returns one part's arrays. A program takes and returns all parts, laid end to end along the dimension named above; an argument that names none is the same for every part. Nothing has to cross between parts.
Inputs may be any that keep to these rules, and one draw needn't show every extreme that they name: The new token takes position cache_lengths; cache positions at or above it are unused. `tile_place`: all 16 entries differ; entries for tiles at or above tile_count name rows that no request uses.
All inputs are finite; a program needn't handle non-finite values.
Results may differ from the reference program's by a relative error of at most 0.009.
Values may be sent and summed in bfloat16 or wider, within the bound.
A program may use at most 128 MiB of HBM per device.

```python
import jax
import jax.numpy as jnp
from jax import lax

D = 8192
HEADS = 64
KV_HEADS = 8
HEAD_DIM = 128
CACHE_SLOTS = 1024
TILE_TOKENS = 320
MAX_TILES = 4
REQUESTS = 4


def draw_cache_lengths(key, part):
    key = jax.random.fold_in(key, 11)
    key = jax.random.fold_in(key, part)
    left_key, right_key, pick_key = jax.random.split(key, 3)
    left_draw = jax.random.randint(left_key, (REQUESTS,), 0, CACHE_SLOTS)
    right_draw = jax.random.randint(right_key, (REQUESTS,), 0, CACHE_SLOTS)
    lengths = 1 + left_draw * right_draw // CACHE_SLOTS
    chosen = jax.random.randint(pick_key, (), 0, REQUESTS)
    return lengths.at[chosen].set(CACHE_SLOTS).astype(jnp.int32)


def draw_tile_count(key, part):
    key = jax.random.fold_in(key, 12)
    key = jax.random.fold_in(key, part)
    count_key, pick_key = jax.random.split(key, 2)
    counts = jax.random.randint(count_key, (REQUESTS,), 1, MAX_TILES + 1)
    chosen = jax.random.randint(pick_key, (), 0, REQUESTS)
    return counts.at[chosen].set(MAX_TILES).astype(jnp.int32)


def draw_tile_place(key, part):
    key = jax.random.fold_in(key, 13)
    order = jax.random.permutation(key, REQUESTS * MAX_TILES)
    return order.reshape(REQUESTS, MAX_TILES).astype(jnp.int32)


def levels(rng, shape, cuts, smallest, largest):
    loudness, own = 1.0, jax.random.fold_in(rng, 6)
    for axis_at, parts in cuts:
        steps = jnp.exp(jax.random.uniform(jax.random.fold_in(own, axis_at), (parts,), jnp.float32, smallest / len(cuts), largest / len(cuts)))
        loudness = loudness * jnp.repeat(steps, shape[axis_at] // parts).reshape([-1 if axis == axis_at else 1 for axis in range(len(shape))])
    return loudness


def centred(key, dims, width, most, pieces=(), held_as=jnp.bfloat16):
    gain = levels(key, dims, pieces, -0.22, 0.18) if pieces else 1.0
    entries = jax.random.normal(key, dims, jnp.float32) * width * gain
    return jnp.minimum(jnp.maximum(entries, -most), most).astype(held_as)


def setup_inputs(seed: int = 0, part: int = 0) -> dict:
    arg_keys = jax.random.split(jax.random.key(seed), 17)
    own_keys = jax.random.split(jax.random.fold_in(arg_keys[16], part), 17)
    return {
        "hidden": centred(own_keys[0], (REQUESTS, D), 1.0, 6.0, ((0, 4),)),
        "self_norm": jnp.clip(1.0 + 0.1 * jax.random.normal(arg_keys[1], (D,), jnp.float32), 0.5, 1.5).astype(jnp.bfloat16),
        "self_query": centred(arg_keys[2], (D, HEADS * HEAD_DIM), D ** -0.5, 0.0625, ((0, 4), (1, 4))),
        "self_keyval": centred(arg_keys[3], (D, 2 * KV_HEADS * HEAD_DIM), D ** -0.5, 0.0625, ((0, 4), (1, 4))),
        "self_output": centred(arg_keys[4], (HEADS * HEAD_DIM, D), (HEADS * HEAD_DIM) ** -0.5, 0.0625, ((0, 4), (1, 4))),
        "key_cache": centred(own_keys[5], (REQUESTS, CACHE_SLOTS, 2 * KV_HEADS * HEAD_DIM), 1.0, 6.0, ((0, 4), (2, 4))),
        "cache_lengths": draw_cache_lengths(jax.random.fold_in(jax.random.fold_in(arg_keys[16], part), 71), part),
        "cross_norm": jnp.clip(1.0 + 0.1 * jax.random.normal(arg_keys[7], (D,), jnp.float32), 0.5, 1.5).astype(jnp.bfloat16),
        "cross_query": centred(arg_keys[8], (D, HEADS * HEAD_DIM), D ** -0.5, 0.0625, ((0, 4), (1, 4))),
        "query_gain": jnp.clip(jax.random.uniform(arg_keys[9], (HEAD_DIM,), jnp.float32, 0.5, 2.0), 0.5, 2.0),
        "key_gain": jnp.clip(jax.random.uniform(arg_keys[10], (HEAD_DIM,), jnp.float32, 0.5, 2.0), 0.5, 2.0),
        "cross_output": centred(arg_keys[11], (HEADS * HEAD_DIM, D), (HEADS * HEAD_DIM) ** -0.5, 0.0625, ((0, 4), (1, 4))),
        "cross_gate": jnp.clip(jax.random.uniform(arg_keys[12], (1,), jnp.float32, 0.3, 1.2), 0.3, 1.2),
        "image_keyval": centred(own_keys[13], (REQUESTS * MAX_TILES, TILE_TOKENS, 2 * KV_HEADS * HEAD_DIM), 1.0, 6.0, ((0, 4), (2, 4))),
        "tile_count": draw_tile_count(jax.random.fold_in(jax.random.fold_in(arg_keys[16], part), 71), part),
        "tile_place": draw_tile_place(jax.random.fold_in(jax.random.fold_in(arg_keys[16], part), 71), part),
    }


EPSILON = 1e-05
THETA = 500000.0

def normalize(values, gains):
    values = values.astype(jnp.float32)
    factor = lax.rsqrt(lax.optimization_barrier(jnp.mean(values * values, axis=-1, keepdims=True)) + EPSILON)
    return values * factor * gains.astype(jnp.float32)

def rotate(values, positions):
    half_dim = values.shape[-1] // 2
    frequency = THETA ** (-(jnp.arange(half_dim, dtype=jnp.float32) * 2.0 / values.shape[-1]))
    angles = positions[:, None] * frequency[None, :]
    cosine = jnp.cos(angles)[:, None, :]
    sine_table = jnp.sin(angles)[:, None, :]
    lower_half = values[..., :half_dim]
    upper_half = values[..., half_dim:]
    return jnp.concatenate([lower_half * cosine - upper_half * sine_table, upper_half * cosine + lower_half * sine_table], axis=-1)

def rounded(values):
    return lax.optimization_barrier(values.astype(jnp.bfloat16)).astype(jnp.float32)

def reference(hidden, self_norm, self_query, self_keyval, self_output, key_cache, cache_lengths, cross_norm, cross_query, query_gain, key_gain, cross_output, cross_gate, image_keyval, tile_count, tile_place):
    requests = hidden.shape[0]
    group_size = HEADS // KV_HEADS
    score_scale = HEAD_DIM ** (-0.5)
    normed = normalize(hidden, self_norm).astype(jnp.bfloat16)
    queries = jnp.dot(normed, self_query, preferred_element_type=jnp.float32).reshape(requests, HEADS, HEAD_DIM)
    fresh_rows = jnp.dot(normed, self_keyval, preferred_element_type=jnp.float32).reshape(requests, KV_HEADS, 2, HEAD_DIM)
    positions = cache_lengths.astype(jnp.float32)
    queries = rotate(queries, positions).astype(jnp.bfloat16)
    fresh_key = rotate(fresh_rows[:, :, 0], positions).astype(jnp.bfloat16)
    fresh_value = fresh_rows[:, :, 1].astype(jnp.bfloat16)
    cache_rows = key_cache.reshape(requests, CACHE_SLOTS, KV_HEADS, 2, HEAD_DIM)
    grouped = queries.reshape(requests, KV_HEADS, group_size, HEAD_DIM).astype(jnp.float32)
    scores = jnp.einsum('rkgd,rtkd->rkgt', grouped, cache_rows[:, :, :, 0].astype(jnp.float32)) * score_scale
    usable = jnp.arange(CACHE_SLOTS)[None, :] < cache_lengths[:, None]
    scores = jnp.where(usable[:, None, None, :], scores, -jnp.inf)
    own_score = jnp.einsum('rkgd,rkd->rkg', grouped, fresh_key.astype(jnp.float32)) * score_scale
    top_score = jnp.maximum(lax.optimization_barrier(jnp.max(scores, axis=-1)), own_score)
    weights = jnp.exp(scores - top_score[..., None])
    own_weight = jnp.exp(own_score - top_score)
    total_weight = lax.optimization_barrier(jnp.sum(weights, axis=-1)) + own_weight
    probabilities = rounded(weights / total_weight[..., None])
    own_prob = rounded(own_weight / total_weight)
    mixed_heads = jnp.einsum('rkgt,rtkd->rkgd', probabilities, cache_rows[:, :, :, 1].astype(jnp.float32))
    mixed_heads = mixed_heads + own_prob[..., None] * fresh_value.astype(jnp.float32)[:, :, None, :]
    attended = mixed_heads.reshape(requests, HEADS * HEAD_DIM).astype(jnp.bfloat16)
    residual = (hidden.astype(jnp.float32) + jnp.dot(attended, self_output, preferred_element_type=jnp.float32)).astype(jnp.bfloat16)
    normed_cross = normalize(residual, cross_norm).astype(jnp.bfloat16)
    cross_queries = jnp.dot(normed_cross, cross_query, preferred_element_type=jnp.float32).reshape(requests, HEADS, HEAD_DIM)
    cross_queries = normalize(cross_queries, query_gain).astype(jnp.bfloat16)

    def one_request(request_item):
        query_row, places, count_in = request_item
        tile_rows = image_keyval[places].reshape(MAX_TILES, TILE_TOKENS, KV_HEADS, 2, HEAD_DIM)
        image_keys = normalize(tile_rows[:, :, :, 0], key_gain).astype(jnp.bfloat16)
        image_values = tile_rows[:, :, :, 1]
        grouped_query = query_row.reshape(KV_HEADS, group_size, HEAD_DIM).astype(jnp.float32)
        tile_scores = jnp.einsum('kgd,jtkd->jkgt', grouped_query, image_keys.astype(jnp.float32)) * score_scale
        tile_top = lax.optimization_barrier(jnp.max(tile_scores, axis=-1))
        tile_exp = jnp.exp(tile_scores - tile_top[..., None])
        tile_sum = lax.optimization_barrier(jnp.sum(tile_exp, axis=-1))
        tile_out = jnp.einsum('jkgt,jtkd->jkgd', rounded(tile_exp), image_values.astype(jnp.float32))
        live_tile = jnp.arange(MAX_TILES) < count_in
        masked_top = jnp.where(live_tile[:, None, None], tile_top, -jnp.inf)
        peak_score = lax.optimization_barrier(jnp.max(masked_top, axis=0))
        factor = jnp.where(live_tile[:, None, None], jnp.exp(tile_top - peak_score[None]), 0.0)
        numerator = lax.optimization_barrier(jnp.sum(factor[..., None] * tile_out, axis=0))
        denominator = lax.optimization_barrier(jnp.sum(factor * tile_sum, axis=0))
        return (numerator / denominator[..., None]).reshape(HEADS * HEAD_DIM)
    crossed = lax.map(one_request, (cross_queries, tile_place, tile_count)).astype(jnp.bfloat16)
    projected = jnp.dot(crossed, cross_output, preferred_element_type=jnp.float32)
    gate_value = jnp.tanh(cross_gate[0])
    return (residual.astype(jnp.float32) + gate_value * projected).astype(jnp.bfloat16)
```

```python
import functools

import jax
import jax.numpy as jnp
from jax import lax
from jax.experimental import pallas as pl
from jax.experimental.pallas import tpu as pltpu
from jax.sharding import PartitionSpec as P

HEAD_DIM = 128
MAX_TILES = 4
EPSILON = 1e-05
THETA = 500000.0
CHUNKS = 4
COLS = 256
LOW = -1e30

F32 = jnp.float32
BF16 = jnp.bfloat16


def kernel(
    dims,
    hidden,
    norms,
    tables,
    lengths,
    gate,
    counts,
    places,
    self_query,
    self_keyval,
    self_output,
    key_cache,
    cross_query,
    cross_output,
    image_keyval,
    out,
    w_sq,
    w_kv,
    w_so,
    w_cq,
    w_co,
    cache,
    image,
    keys,
    h_send,
    h_recv,
    p_send,
    p_recv,
    a_send,
    a_recv,
    s_send,
    s_recv,
    c_part,
    c_send,
    c_recv,
    o_send,
    o_recv,
    x_send,
    x_recv,
    f_send,
    f_recv,
    lhs,
    factor_rep,
    load_sem,
    send_sem,
    recv_sem,
):
    batch, tensor, width, kv_width, model, tokens = dims
    requests = batch
    depth = model // batch
    heads = width // HEAD_DIM
    kv_heads = kv_width // (2 * HEAD_DIM)
    group = heads // kv_heads
    slots = image_keyval.shape[0]
    scale = HEAD_DIM ** (-0.5)
    me = lax.axis_index("batch")
    mine = lax.axis_index("tensor")

    loads = {}

    def load(name, source, target, at, pieces=CHUNKS):
        rows = source.shape[0] // pieces
        loads[name] = [
            pltpu.make_async_copy(
                source.at[pl.ds(i * rows, rows)],
                target.at[pl.ds(i * rows, rows)],
                load_sem.at[at + i],
            )
            for i in range(pieces)
        ]

    load("sq", self_query, w_sq, 0)
    load("kv", self_keyval, w_kv, CHUNKS)
    load("so", self_output, w_so, 2 * CHUNKS)
    load("cq", cross_query, w_cq, 3 * CHUNKS)
    load("co", cross_output, w_co, 4 * CHUNKS)
    load("cache", key_cache.at[0], cache, 5 * CHUNKS)
    loads["image"] = [
        pltpu.make_async_copy(
            image_keyval.at[s], image.at[pl.ds(s * tokens, tokens)], load_sem.at[6 * CHUNKS + s]
        )
        for s in range(slots)
    ]

    def start(*names):
        for name in names:
            for copy in loads[name]:
                copy.start()

    def arrive(*names):
        for name in names:
            for copy in loads[name]:
                copy.wait()

    start("sq", "kv", "cache")

    barrier = pltpu.get_barrier_semaphore()
    for d in range(1, batch):
        pl.semaphore_signal(
            barrier,
            inc=1,
            device_id={"batch": lax.rem(me + d, batch)},
            device_id_type=pl.DeviceIdType.MESH,
        )
    for d in range(1, tensor):
        pl.semaphore_signal(
            barrier,
            inc=1,
            device_id={"tensor": lax.rem(mine + d, tensor)},
            device_id_type=pl.DeviceIdType.MESH,
        )
    for j in range(batch):
        h_send[j] = hidden[:, j * depth : (j + 1) * depth].astype(F32)
    h_recv[me] = h_send[me]
    pl.semaphore_wait(barrier, batch + tensor - 2)

    pending = []

    def exchange(phase, axis, count, index, source, target):
        copies = []
        for d in range(1, count):
            to = lax.rem(index + d, count)
            copy = pltpu.make_async_remote_copy(
                src_ref=source(to),
                dst_ref=target.at[index],
                send_sem=send_sem.at[phase, d],
                recv_sem=recv_sem.at[phase, d],
                device_id={axis: to},
                device_id_type=pl.DeviceIdType.MESH,
            )
            copy.start()
            copies.append(copy)
        pending.extend(copies)
        return copies

    def received(copies):
        for copy in copies:
            copy.wait_recv()

    def total(ref, count):
        value = ref[0]
        for j in range(1, count):
            value = value + ref[j]
        return value

    def multiply(left, weight, columns, store):
        @pl.loop(0, columns // COLS)
        def _(i):
            part = jnp.dot(
                left, weight[:, pl.ds(pl.multiple_of(i * COLS, COLS), COLS)],
                preferred_element_type=F32,
            )
            store(i, part)

    per_tile = COLS // HEAD_DIM

    copies = exchange(0, "batch", batch, me, lambda to: h_send.at[to], h_recv)
    received(copies)
    for r in range(requests):
        lhs[pl.ds(r, 1), 0:depth] = h_recv[r]
    hidden_cols = lhs[:, 0:depth]
    squares = jnp.sum(hidden_cols * hidden_cols, axis=1, keepdims=True)
    left = (hidden_cols * norms[0:1, :]).astype(BF16)

    qkv_rows = heads + 2 * kv_heads

    def store_rows(base):
        def store(i, part):
            for r in range(requests):
                for c in range(per_tile):
                    p_send[r, pl.ds(base + i * per_tile + c, 1), :] = part[
                        r : r + 1, c * HEAD_DIM : (c + 1) * HEAD_DIM
                    ]

        return store

    for r in range(requests):
        p_send[r, pl.ds(qkv_rows, 1), :] = jnp.broadcast_to(squares[r : r + 1], (1, HEAD_DIM))
    arrive("sq", "kv")
    start("so", "image", "cq", "co")
    multiply(left, w_sq, width, store_rows(0))
    multiply(left, w_kv, kv_width, store_rows(heads))
    p_recv[me] = p_send[me]
    copies = exchange(1, "batch", batch, me, lambda to: p_send.at[to], p_recv)
    arrive("cache")
    received(copies)
    projected = total(p_recv, batch)
    factor = lax.rsqrt(projected[qkv_rows : qkv_rows + 1] * (1.0 / model) + EPSILON)
    projected = projected * factor
    rotated = projected * tables[0:1, :] + pltpu.roll(projected, HEAD_DIM // 2, 1) * tables[1:2, :]

    position = lax.broadcasted_iota(jnp.int32, (group, cache.shape[0]), 1)
    usable = position < lengths[0]
    for k in range(kv_heads):
        query = rotated[k * group : (k + 1) * group].astype(BF16)
        at = heads + 2 * k
        fresh_key = rotated[at : at + 1].astype(BF16).astype(F32)
        fresh_value = projected[at + 1 : at + 2].astype(BF16).astype(F32)
        base = 2 * k * HEAD_DIM
        scores = (
            lax.dot_general(
                query,
                cache[:, base : base + HEAD_DIM],
                (((1,), (1,)), ((), ())),
                preferred_element_type=F32,
            )
            * scale
        )
        scores = jnp.where(usable, scores, LOW)
        own_score = jnp.sum(query.astype(F32) * fresh_key, axis=1, keepdims=True) * scale
        top = jnp.maximum(jnp.max(scores, axis=1, keepdims=True), own_score)
        weights = jnp.exp(scores - top)
        own_weight = jnp.exp(own_score - top)
        inverse = 1.0 / (jnp.sum(weights, axis=1, keepdims=True) + own_weight)
        mixed = jnp.dot(
            (weights * inverse).astype(BF16),
            cache[:, base + HEAD_DIM : base + 2 * HEAD_DIM],
            preferred_element_type=F32,
        )
        own_prob = (own_weight * inverse).astype(BF16).astype(F32)
        a_send[k * group : (k + 1) * group, :] = mixed + own_prob * fresh_value
    a_recv[me] = a_send[...]
    copies = exchange(2, "batch", batch, me, lambda to: a_send, a_recv)
    first = me * slots
    owners = [jnp.int32(-1)] * slots
    for r in range(requests):
        for j in range(MAX_TILES):
            at = jnp.where(j < counts[r], places[r, j] - first, -1)
            owners = [jnp.where(at == s, r, owner) for s, owner in enumerate(owners)]
    arrive("so")
    received(copies)

    for h in range(heads):
        lhs[:, h * HEAD_DIM : (h + 1) * HEAD_DIM] = a_recv[:, h, :]
    left = lhs[:, 0:width].astype(BF16)

    def store_columns(target):
        def store(i, part):
            target[:, pl.ds(pl.multiple_of(i * COLS, COLS), COLS)] = part

        return store

    multiply(left, w_so, depth, store_columns(s_send))
    s_recv[mine] = s_send[...]
    copies = exchange(3, "tensor", tensor, mine, lambda to: s_send, s_recv)

    arrive("image")
    for k in range(kv_heads):
        base = 2 * k * HEAD_DIM
        for s in range(slots):
            rows = slice(s * tokens, (s + 1) * tokens)
            raw = image[rows, base : base + HEAD_DIM].astype(F32)
            inverse = lax.rsqrt(jnp.mean(raw * raw, axis=1, keepdims=True) + EPSILON)
            keys[k, rows, :] = (raw * inverse * tables[3:4, :]).astype(BF16)
    arrive("cq")
    received(copies)
    residual = (hidden_cols + total(s_recv, tensor)).astype(BF16).astype(F32)
    squares = jnp.sum(residual * residual, axis=1, keepdims=True)
    left = (residual * norms[1:2, :]).astype(BF16)

    def store_heads(i, part):
        for c in range(per_tile):
            c_part[i * per_tile + c] = part[:, c * HEAD_DIM : (c + 1) * HEAD_DIM]

    multiply(left, w_cq, width, store_heads)
    for h in range(heads):
        c_send[h * requests : (h + 1) * requests, :] = c_part[h]
    c_send[heads * requests : (heads + 1) * requests, :] = jnp.broadcast_to(
        squares, (requests, HEAD_DIM)
    )
    c_recv[me] = c_send[...]
    copies = exchange(4, "batch", batch, me, lambda to: c_send, c_recv)
    received(copies)
    raw = total(c_recv, batch)
    factor = lax.rsqrt(
        raw[heads * requests : (heads + 1) * requests] * (1.0 / model) + EPSILON
    )
    for h in range(heads):
        factor_rep[h * requests : (h + 1) * requests, :] = factor
    raw = raw[0 : heads * requests] * factor_rep[...]
    inverse = lax.rsqrt(jnp.mean(raw * raw, axis=1, keepdims=True) + EPSILON)
    queries = (raw * inverse * tables[2:3, :]).astype(BF16)

    shape = (group * requests, slots * tokens)
    column = lax.broadcasted_iota(jnp.int32, shape, 1)
    owner = jnp.full(shape, owners[0])
    for s in range(1, slots):
        owner = jnp.where(column >= s * tokens, owners[s], owner)
    mask = lax.rem(lax.broadcasted_iota(jnp.int32, shape, 0), requests) == owner
    lane = lax.broadcasted_iota(jnp.int32, (group * requests, HEAD_DIM), 1)
    stats = jnp.zeros((group * requests, HEAD_DIM), F32)
    for k in range(kv_heads):
        base = (2 * k + 1) * HEAD_DIM
        rows = slice(k * group * requests, (k + 1) * group * requests)
        scores = (
            lax.dot_general(
                queries[rows], keys[k], (((1,), (1,)), ((), ())), preferred_element_type=F32
            )
            * scale
        )
        scores = jnp.where(mask, scores, LOW)
        top = jnp.max(scores, axis=1, keepdims=True)
        weights = jnp.where(mask, jnp.exp(scores - top), 0.0)
        amount = jnp.sum(weights, axis=1, keepdims=True)
        o_send[k] = jnp.dot(
            weights.astype(BF16), image[:, base : base + HEAD_DIM], preferred_element_type=F32
        )
        stats = jnp.where(lane == 2 * k, top, stats)
        stats = jnp.where(lane == 2 * k + 1, amount, stats)
    o_send[kv_heads] = stats
    o_recv[me] = o_send[...]
    copies = exchange(5, "batch", batch, me, lambda to: o_send, o_recv)
    arrive("co")
    received(copies)
    for k in range(kv_heads):
        tops = [o_recv[j, kv_heads, :, 2 * k : 2 * k + 1] for j in range(batch)]
        peak = functools.reduce(jnp.maximum, tops)
        factors = [jnp.exp(top - peak) for top in tops]
        amount = sum(
            f * o_recv[j, kv_heads, :, 2 * k + 1 : 2 * k + 2] for j, f in enumerate(factors)
        )
        crossed = sum(f * o_recv[j, k] for j, f in enumerate(factors)) / amount
        for g in range(group):
            h = k * group + g
            lhs[:, h * HEAD_DIM : (h + 1) * HEAD_DIM] = crossed[g * requests : (g + 1) * requests]
    left = lhs[:, 0:width].astype(BF16)

    multiply(left, w_co, depth, store_columns(x_send))
    x_recv[mine] = x_send[...]
    copies = exchange(6, "tensor", tensor, mine, lambda to: x_send, x_recv)
    amount = jnp.tanh(jnp.full((1, HEAD_DIM), gate[0]))[:, 0:1]
    received(copies)
    final = residual + amount * total(x_recv, tensor)
    for r in range(requests):
        f_send[r] = final[r : r + 1]
    f_recv[me] = f_send[me]
    copies = exchange(7, "batch", batch, me, lambda to: f_send.at[to], f_recv)
    received(copies)
    for j in range(batch):
        out[:, j * depth : (j + 1) * depth] = f_recv[j].astype(BF16)
    for copy in pending:
        copy.wait_send()


def per_device(
    hidden,
    self_norm,
    self_query,
    self_keyval,
    self_output,
    key_cache,
    cache_lengths,
    cross_norm,
    cross_query,
    query_gain,
    key_gain,
    cross_output,
    cross_gate,
    image_keyval,
    tile_count,
    tile_place,
):
    batch = lax.axis_size("batch")
    tensor = lax.axis_size("tensor")
    assert hidden.shape[0] == 1
    model = hidden.shape[1]
    depth = model // batch
    width = self_query.shape[1]
    kv_width = self_keyval.shape[1]
    heads = width // HEAD_DIM
    kv_heads = kv_width // (2 * HEAD_DIM)
    group = heads // kv_heads
    slots, tokens = image_keyval.shape[:2]
    requests = batch

    half = HEAD_DIM // 2
    frequency = THETA ** (-(jnp.arange(half, dtype=F32) * 2.0 / HEAD_DIM))
    angles = cache_lengths.astype(F32)[:, None] * frequency[None, :]
    cosine, sine = jnp.cos(angles), jnp.sin(angles)
    tables = jnp.concatenate(
        [
            jnp.concatenate([cosine, cosine], axis=1),
            jnp.concatenate([-sine, sine], axis=1),
            query_gain[None],
            key_gain[None],
        ],
        axis=0,
    )
    at = lax.axis_index("batch") * depth
    norms = jnp.stack(
        [lax.dynamic_slice(self_norm, (at,), (depth,)), lax.dynamic_slice(cross_norm, (at,), (depth,))]
    ).astype(F32)

    vmem = pl.BlockSpec(memory_space=pltpu.VMEM)
    smem = pl.BlockSpec(memory_space=pltpu.SMEM)
    anywhere = pl.BlockSpec(memory_space=pl.ANY)
    qkv_rows = -(-(heads + 2 * kv_heads + 1) // 8) * 8
    cross_rows = (heads + 1) * requests
    cross_rows = -(-cross_rows // 8) * 8
    dims = (batch, tensor, width, kv_width, model, tokens)
    return pl.pallas_call(
        functools.partial(kernel, dims),
        out_shape=jax.ShapeDtypeStruct((1, model), BF16),
        in_specs=[vmem] * 3 + [smem] * 4 + [anywhere] * 7,
        out_specs=vmem,
        scratch_shapes=[
            pltpu.VMEM(self_query.shape, BF16),
            pltpu.VMEM(self_keyval.shape, BF16),
            pltpu.VMEM(self_output.shape, BF16),
            pltpu.VMEM(cross_query.shape, BF16),
            pltpu.VMEM(cross_output.shape, BF16),
            pltpu.VMEM(key_cache.shape[1:], BF16),
            pltpu.VMEM((slots * tokens, kv_width), BF16),
            pltpu.VMEM((kv_heads, slots * tokens, HEAD_DIM), BF16),
            pltpu.VMEM((batch, 1, depth), F32),
            pltpu.VMEM((batch, 1, depth), F32),
            pltpu.VMEM((batch, qkv_rows, HEAD_DIM), F32),
            pltpu.VMEM((batch, qkv_rows, HEAD_DIM), F32),
            pltpu.VMEM((heads, HEAD_DIM), F32),
            pltpu.VMEM((batch, heads, HEAD_DIM), F32),
            pltpu.VMEM((requests, depth), F32),
            pltpu.VMEM((tensor, requests, depth), F32),
            pltpu.VMEM((heads, requests, HEAD_DIM), F32),
            pltpu.VMEM((cross_rows, HEAD_DIM), F32),
            pltpu.VMEM((batch, cross_rows, HEAD_DIM), F32),
            pltpu.VMEM((kv_heads + 1, group * requests, HEAD_DIM), F32),
            pltpu.VMEM((batch, kv_heads + 1, group * requests, HEAD_DIM), F32),
            pltpu.VMEM((requests, depth), F32),
            pltpu.VMEM((tensor, requests, depth), F32),
            pltpu.VMEM((batch, 1, depth), F32),
            pltpu.VMEM((batch, 1, depth), F32),
            pltpu.VMEM((requests, max(width, depth)), F32),
            pltpu.VMEM((heads * requests, HEAD_DIM), F32),
            pltpu.SemaphoreType.DMA((6 * CHUNKS + slots,)),
            pltpu.SemaphoreType.DMA((8, max(batch, tensor))),
            pltpu.SemaphoreType.DMA((8, max(batch, tensor))),
        ],
        compiler_params=pltpu.CompilerParams(
            collective_id=0, has_side_effects=True, vmem_limit_bytes=56 * 1024 * 1024
        ),
    )(
        hidden,
        norms,
        tables,
        cache_lengths,
        cross_gate,
        tile_count,
        tile_place,
        self_query,
        self_keyval,
        self_output,
        key_cache,
        cross_query,
        cross_output,
        image_keyval,
    )


def solution(mesh):
    in_specs = (
        P(("groups", "batch"), None),
        P(),
        P("batch", "tensor"),
        P("batch", "tensor"),
        P("tensor", "batch"),
        P(("groups", "batch"), None, "tensor"),
        P(("groups", "batch")),
        P(),
        P("batch", "tensor"),
        P(),
        P(),
        P("tensor", "batch"),
        P(),
        P(("groups", "batch"), None, "tensor"),
        P("groups"),
        P("groups", None),
    )
    out_specs = P(("groups", "batch"), None)
    return jax.shard_map(
        per_device, mesh=mesh, in_specs=in_specs, out_specs=out_specs, check_vma=False
    )
```

```python
import functools

import jax
import jax.numpy as jnp
from jax import lax
from jax.experimental import pallas as pl
from jax.experimental.pallas import tpu as pltpu
from jax.sharding import PartitionSpec as P

HEAD_DIM = 128
MAX_TILES = 4
EPSILON = 1e-05
THETA = 500000.0
CHUNKS = 4
COLS = 256
LOW = -1e30

F32 = jnp.float32
BF16 = jnp.bfloat16


def kernel(
    dims,
    hidden,
    self_norm,
    cross_norm,
    cosine,
    sine,
    query_gain,
    key_gain,
    lengths,
    gate,
    counts,
    places,
    self_query,
    self_keyval,
    self_output,
    key_cache,
    cross_query,
    cross_output,
    image_keyval,
    out,
    w_sq,
    w_kv,
    w_so,
    w_cq,
    w_co,
    cache,
    image,
    keys,
    h_send,
    h_recv,
    p_send,
    p_recv,
    a_send,
    a_recv,
    parts,
    stage,
    s_send,
    s_recv,
    c_stage,
    c_send,
    c_recv,
    o_send,
    o_recv,
    x_send,
    x_recv,
    f_send,
    f_recv,
    lhs,
    factor_rep,
    norm_rows,
    trig,
    a_rows,
    load_sem,
    send_sem,
    recv_sem,
):
    batch, tensor, width, kv_width, model, tokens = dims
    requests = batch
    depth = model // batch
    heads = width // HEAD_DIM
    kv_heads = kv_width // (2 * HEAD_DIM)
    group = heads // kv_heads
    slots = image_keyval.shape[0]
    scale = HEAD_DIM ** (-0.5)
    me = lax.axis_index("batch")
    mine = lax.axis_index("tensor")

    loads = {}

    def load(name, source, target, at, pieces=CHUNKS):
        rows = source.shape[0] // pieces
        loads[name] = [
            pltpu.make_async_copy(
                source.at[pl.ds(i * rows, rows)],
                target.at[pl.ds(i * rows, rows)],
                load_sem.at[at + i],
            )
            for i in range(pieces)
        ]

    load("sq", self_query, w_sq, 0)
    load("kv", self_keyval, w_kv, CHUNKS)
    load("so", self_output, w_so, 2 * CHUNKS)
    load("cq", cross_query, w_cq, 3 * CHUNKS)
    load("co", cross_output, w_co, 4 * CHUNKS)
    load("cache", key_cache.at[0], cache, 5 * CHUNKS)
    loads["image"] = [
        pltpu.make_async_copy(
            image_keyval.at[s], image.at[pl.ds(s * tokens, tokens)], load_sem.at[6 * CHUNKS + s]
        )
        for s in range(slots)
    ]

    def start(*names):
        for name in names:
            for copy in loads[name]:
                copy.start()

    def arrive(*names):
        for name in names:
            for copy in loads[name]:
                copy.wait()

    start("sq", "kv", "cache")

    barrier = pltpu.get_barrier_semaphore()
    for d in range(1, batch):
        pl.semaphore_signal(
            barrier,
            inc=1,
            device_id={"batch": lax.rem(me + d, batch)},
            device_id_type=pl.DeviceIdType.MESH,
        )
    for d in range(1, tensor):
        pl.semaphore_signal(
            barrier,
            inc=1,
            device_id={"tensor": lax.rem(mine + d, tensor)},
            device_id_type=pl.DeviceIdType.MESH,
        )
    for j in range(batch):
        columns = slice(j * depth, (j + 1) * depth)
        h_send[j] = hidden[:, columns].astype(F32)
        norm_rows[0, j] = self_norm[:, columns].astype(F32)
        norm_rows[1, j] = cross_norm[:, columns].astype(F32)
    h_recv[me] = h_send[me]
    half = HEAD_DIM // 2
    trig[0:1, 0:half] = cosine[...]
    trig[0:1, half:HEAD_DIM] = cosine[...]
    trig[1:2, 0:half] = -sine[...]
    trig[1:2, half:HEAD_DIM] = sine[...]
    pl.semaphore_wait(barrier, batch + tensor - 2)

    pending = []

    def exchange(phase, axis, count, index, source, target):
        copies = []
        for d in range(1, count):
            to = lax.rem(index + d, count)
            copy = pltpu.make_async_remote_copy(
                src_ref=source(to),
                dst_ref=target.at[index],
                send_sem=send_sem.at[phase, d],
                recv_sem=recv_sem.at[phase, d],
                device_id={axis: to},
                device_id_type=pl.DeviceIdType.MESH,
            )
            copy.start()
            copies.append(copy)
        pending.extend(copies)
        return copies

    def received(copies):
        for copy in copies:
            copy.wait_recv()

    def total(ref, count):
        value = ref[0].astype(F32)
        for j in range(1, count):
            value = value + ref[j].astype(F32)
        return value

    def thirds(value):
        high = value.astype(BF16).astype(F32)
        middle = (value - high).astype(BF16).astype(F32)
        return high, middle, value - high - middle

    def multiply(left, weight, columns, store):
        @pl.loop(0, columns // COLS)
        def _(i):
            part = jnp.dot(
                left, weight[:, pl.ds(pl.multiple_of(i * COLS, COLS), COLS)],
                preferred_element_type=F32,
            )
            store(i, part)

    per_tile = COLS // HEAD_DIM

    copies = exchange(0, "batch", batch, me, lambda to: h_send.at[to], h_recv)
    received(copies)
    for r in range(requests):
        lhs[pl.ds(r, 1), 0:depth] = h_recv[r]
    hidden_cols = lhs[:, 0:depth]
    squares = jnp.sum(hidden_cols * hidden_cols, axis=1, keepdims=True)
    left = (hidden_cols * norm_rows[0, me]).astype(BF16)

    qkv_rows = heads + 2 * kv_heads

    def store_rows(base):
        def store(i, part):
            for r in range(requests):
                for c in range(per_tile):
                    p_send[r, pl.ds(base + i * per_tile + c, 1), :] = part[
                        r : r + 1, c * HEAD_DIM : (c + 1) * HEAD_DIM
                    ]

        return store

    for r in range(requests):
        p_send[r, pl.ds(qkv_rows, 1), :] = jnp.broadcast_to(squares[r : r + 1], (1, HEAD_DIM))
    arrive("sq", "kv")
    start("so", "image", "cq", "co")
    multiply(left, w_sq, width, store_rows(0))
    multiply(left, w_kv, kv_width, store_rows(heads))
    p_recv[me] = p_send[me]
    copies = exchange(1, "batch", batch, me, lambda to: p_send.at[to], p_recv)
    arrive("cache")
    received(copies)
    projected = total(p_recv, batch)
    factor = lax.rsqrt(projected[qkv_rows : qkv_rows + 1] * (1.0 / model) + EPSILON)
    projected = projected * factor
    rotated = projected * trig[0:1, :] + pltpu.roll(projected, HEAD_DIM // 2, 1) * trig[1:2, :]

    position = lax.broadcasted_iota(jnp.int32, (group, cache.shape[0]), 1)
    usable = position < lengths[0]
    for k in range(kv_heads):
        query = rotated[k * group : (k + 1) * group].astype(BF16)
        at = heads + 2 * k
        fresh_key = rotated[at : at + 1].astype(BF16).astype(F32)
        fresh_value = projected[at + 1 : at + 2].astype(BF16).astype(F32)
        base = 2 * k * HEAD_DIM
        scores = (
            lax.dot_general(
                query,
                cache[:, base : base + HEAD_DIM],
                (((1,), (1,)), ((), ())),
                preferred_element_type=F32,
            )
            * scale
        )
        scores = jnp.where(usable, scores, LOW)
        own_score = jnp.sum(query.astype(F32) * fresh_key, axis=1, keepdims=True) * scale
        top = jnp.maximum(jnp.max(scores, axis=1, keepdims=True), own_score)
        weights = jnp.exp(scores - top)
        own_weight = jnp.exp(own_score - top)
        inverse = 1.0 / (jnp.sum(weights, axis=1, keepdims=True) + own_weight)
        mixed = jnp.dot(
            (weights * inverse).astype(BF16),
            cache[:, base + HEAD_DIM : base + 2 * HEAD_DIM],
            preferred_element_type=F32,
        )
        own_prob = (own_weight * inverse).astype(BF16).astype(F32)
        a_rows[0, k * group : (k + 1) * group, :] = mixed + own_prob * fresh_value
    a_send[...] = a_rows[0].astype(BF16)
    a_recv[me] = a_send[...]
    copies = exchange(2, "batch", batch, me, lambda to: a_send, a_recv)
    first = me * slots
    owners = [jnp.int32(-1)] * slots
    for r in range(requests):
        for j in range(MAX_TILES):
            at = jnp.where(j < counts[r], places[r, j] - first, -1)
            owners = [jnp.where(at == s, r, owner) for s, owner in enumerate(owners)]
    arrive("so")
    received(copies)

    for r in range(requests):
        a_rows[r] = a_recv[r].astype(F32)
    for h in range(heads):
        lhs[:, h * HEAD_DIM : (h + 1) * HEAD_DIM] = a_rows[:, h, :]
    left = lhs[:, 0:width].astype(BF16)

    blocks = depth // HEAD_DIM

    def store_blocks(i, part):
        for c in range(per_tile):
            parts[i * per_tile + c] = part[:, c * HEAD_DIM : (c + 1) * HEAD_DIM]

    def pack(target):
        for c in range(blocks):
            stage[c * requests : (c + 1) * requests, :] = parts[c]
        target[...] = stage[...].astype(BF16)

    def unpack(ref):
        rows = total(ref, tensor)
        for c in range(blocks):
            lhs[:, c * HEAD_DIM : (c + 1) * HEAD_DIM] = rows[c * requests : (c + 1) * requests]
        return lhs[:, 0:depth]

    multiply(left, w_so, depth, store_blocks)
    pack(s_send)
    s_recv[mine] = s_send[...]
    copies = exchange(3, "tensor", tensor, mine, lambda to: s_send, s_recv)

    arrive("image")
    for k in range(kv_heads):
        base = 2 * k * HEAD_DIM
        for s in range(slots):
            rows = slice(s * tokens, (s + 1) * tokens)
            raw = image[rows, base : base + HEAD_DIM].astype(F32)
            inverse = lax.rsqrt(jnp.mean(raw * raw, axis=1, keepdims=True) + EPSILON)
            keys[k, rows, :] = (raw * inverse * key_gain[...]).astype(BF16)
    arrive("cq")
    received(copies)
    residual = (hidden_cols + unpack(s_recv)).astype(BF16).astype(F32)
    squares = jnp.sum(residual * residual, axis=1, keepdims=True)
    left = (residual * norm_rows[1, me]).astype(BF16)

    multiply(left, w_cq, width, store_blocks)
    for h in range(heads):
        c_stage[h * requests : (h + 1) * requests, :] = parts[h]
    lane = lax.broadcasted_iota(jnp.int32, (requests, HEAD_DIM), 1)
    split = jnp.zeros((requests, HEAD_DIM), F32)
    for i, third in enumerate(thirds(squares)):
        split = jnp.where(lane == i, third, split)
    rest = c_stage.shape[0] - heads * requests
    c_stage[heads * requests :, :] = jnp.zeros((rest, HEAD_DIM), F32)
    c_stage[heads * requests : (heads + 1) * requests, :] = split
    c_send[...] = c_stage[...].astype(BF16)
    c_recv[me] = c_send[...]
    copies = exchange(4, "batch", batch, me, lambda to: c_send, c_recv)
    received(copies)
    raw = total(c_recv, batch)
    squares = jnp.sum(raw[heads * requests : (heads + 1) * requests], axis=1, keepdims=True)
    factor = lax.rsqrt(squares * (1.0 / model) + EPSILON)
    factor = jnp.broadcast_to(factor, (requests, HEAD_DIM))
    for h in range(heads):
        factor_rep[h * requests : (h + 1) * requests, :] = factor
    raw = raw[0 : heads * requests] * factor_rep[...]
    inverse = lax.rsqrt(jnp.mean(raw * raw, axis=1, keepdims=True) + EPSILON)
    queries = (raw * inverse * query_gain[...]).astype(BF16)

    shape = (group * requests, slots * tokens)
    column = lax.broadcasted_iota(jnp.int32, shape, 1)
    owner = jnp.full(shape, owners[0])
    for s in range(1, slots):
        owner = jnp.where(column >= s * tokens, owners[s], owner)
    mask = lax.rem(lax.broadcasted_iota(jnp.int32, shape, 0), requests) == owner
    lane = lax.broadcasted_iota(jnp.int32, (group * requests, HEAD_DIM), 1)
    stats = jnp.zeros((group * requests, HEAD_DIM), F32)
    for k in range(kv_heads):
        base = (2 * k + 1) * HEAD_DIM
        rows = slice(k * group * requests, (k + 1) * group * requests)
        scores = (
            lax.dot_general(
                queries[rows], keys[k], (((1,), (1,)), ((), ())), preferred_element_type=F32
            )
            * scale
        )
        scores = jnp.where(mask, scores, LOW)
        top = jnp.max(scores, axis=1, keepdims=True)
        weights = jnp.where(mask, jnp.exp(scores - top), 0.0)
        amount = jnp.sum(weights, axis=1, keepdims=True)
        o_send[k] = jnp.dot(
            weights.astype(BF16), image[:, base : base + HEAD_DIM], preferred_element_type=F32
        ).astype(BF16)
        for i, third in enumerate(thirds(top) + thirds(amount)):
            stats = jnp.where(lane == 6 * k + i, third, stats)
    o_send[kv_heads] = stats.astype(BF16)
    o_recv[me] = o_send[...]
    copies = exchange(5, "batch", batch, me, lambda to: o_send, o_recv)
    arrive("co")
    received(copies)
    for k in range(kv_heads):
        at = 6 * k
        blocks_in = [o_recv[j, kv_heads].astype(F32) for j in range(batch)]
        tops, sums = [
            [
                b[:, i : i + 1] + b[:, i + 1 : i + 2] + b[:, i + 2 : i + 3]
                for b in blocks_in
            ]
            for i in (at, at + 3)
        ]
        peak = functools.reduce(jnp.maximum, tops)
        factors = [jnp.exp(top - peak) for top in tops]
        amount = sum(f * part for f, part in zip(factors, sums))
        crossed = sum(f * o_recv[j, k].astype(F32) for j, f in enumerate(factors)) / amount
        for g in range(group):
            h = k * group + g
            lhs[:, h * HEAD_DIM : (h + 1) * HEAD_DIM] = crossed[g * requests : (g + 1) * requests]
    left = lhs[:, 0:width].astype(BF16)

    multiply(left, w_co, depth, store_blocks)
    pack(x_send)
    x_recv[mine] = x_send[...]
    copies = exchange(6, "tensor", tensor, mine, lambda to: x_send, x_recv)
    gating = jnp.tanh(jnp.full((1, HEAD_DIM), gate[0]))[:, 0:1]
    received(copies)
    final = residual + gating * unpack(x_recv)
    for r in range(requests):
        f_send[r] = final[r : r + 1]
    f_recv[me] = f_send[me]
    copies = exchange(7, "batch", batch, me, lambda to: f_send.at[to], f_recv)
    received(copies)
    for j in range(batch):
        out[:, j * depth : (j + 1) * depth] = f_recv[j]
    for copy in pending:
        copy.wait_send()


def per_device(
    hidden,
    self_norm,
    self_query,
    self_keyval,
    self_output,
    key_cache,
    cache_lengths,
    cross_norm,
    cross_query,
    query_gain,
    key_gain,
    cross_output,
    cross_gate,
    image_keyval,
    tile_count,
    tile_place,
):
    batch = lax.axis_size("batch")
    tensor = lax.axis_size("tensor")
    assert hidden.shape[0] == 1
    model = hidden.shape[1]
    depth = model // batch
    width = self_query.shape[1]
    kv_width = self_keyval.shape[1]
    heads = width // HEAD_DIM
    kv_heads = kv_width // (2 * HEAD_DIM)
    group = heads // kv_heads
    slots, tokens = image_keyval.shape[:2]
    requests = batch

    half = HEAD_DIM // 2
    frequency = THETA ** (-(jnp.arange(half, dtype=F32) * 2.0 / HEAD_DIM))
    angles = cache_lengths.astype(F32)[:, None] * frequency[None, :]
    cosine, sine = jnp.cos(angles), jnp.sin(angles)
    vmem = pl.BlockSpec(memory_space=pltpu.VMEM)
    smem = pl.BlockSpec(memory_space=pltpu.SMEM)
    anywhere = pl.BlockSpec(memory_space=pl.ANY)
    qkv_rows = -(-(heads + 2 * kv_heads + 1) // 8) * 8
    cross_rows = -(-(heads + 1) * requests // 16) * 16
    head_rows = -(-heads // 16) * 16
    blocks = depth // HEAD_DIM
    sum_rows = blocks * requests
    dims = (batch, tensor, width, kv_width, model, tokens)
    result = pl.pallas_call(
        functools.partial(kernel, dims),
        out_shape=jax.ShapeDtypeStruct((1, model), F32),
        in_specs=[vmem] * 7 + [smem] * 4 + [anywhere] * 7,
        out_specs=vmem,
        scratch_shapes=[
            pltpu.VMEM(self_query.shape, BF16),
            pltpu.VMEM(self_keyval.shape, BF16),
            pltpu.VMEM(self_output.shape, BF16),
            pltpu.VMEM(cross_query.shape, BF16),
            pltpu.VMEM(cross_output.shape, BF16),
            pltpu.VMEM(key_cache.shape[1:], BF16),
            pltpu.VMEM((slots * tokens, kv_width), BF16),
            pltpu.VMEM((kv_heads, slots * tokens, HEAD_DIM), BF16),
            pltpu.VMEM((batch, 1, depth), F32),
            pltpu.VMEM((batch, 1, depth), F32),
            pltpu.VMEM((batch, qkv_rows, HEAD_DIM), F32),
            pltpu.VMEM((batch, qkv_rows, HEAD_DIM), F32),
            pltpu.VMEM((head_rows, HEAD_DIM), BF16),
            pltpu.VMEM((batch, head_rows, HEAD_DIM), BF16),
            pltpu.VMEM((max(heads, blocks), requests, HEAD_DIM), F32),
            pltpu.VMEM((sum_rows, HEAD_DIM), F32),
            pltpu.VMEM((sum_rows, HEAD_DIM), BF16),
            pltpu.VMEM((tensor, sum_rows, HEAD_DIM), BF16),
            pltpu.VMEM((cross_rows, HEAD_DIM), F32),
            pltpu.VMEM((cross_rows, HEAD_DIM), BF16),
            pltpu.VMEM((batch, cross_rows, HEAD_DIM), BF16),
            pltpu.VMEM((kv_heads + 1, group * requests, HEAD_DIM), BF16),
            pltpu.VMEM((batch, kv_heads + 1, group * requests, HEAD_DIM), BF16),
            pltpu.VMEM((sum_rows, HEAD_DIM), BF16),
            pltpu.VMEM((tensor, sum_rows, HEAD_DIM), BF16),
            pltpu.VMEM((batch, 1, depth), F32),
            pltpu.VMEM((batch, 1, depth), F32),
            pltpu.VMEM((requests, max(width, depth)), F32),
            pltpu.VMEM((heads * requests, HEAD_DIM), F32),
            pltpu.VMEM((2, batch, 1, depth), F32),
            pltpu.VMEM((8, HEAD_DIM), F32),
            pltpu.VMEM((batch, head_rows, HEAD_DIM), F32),
            pltpu.SemaphoreType.DMA((6 * CHUNKS + slots,)),
            pltpu.SemaphoreType.DMA((8, max(batch, tensor))),
            pltpu.SemaphoreType.DMA((8, max(batch, tensor))),
        ],
        compiler_params=pltpu.CompilerParams(
            collective_id=0, has_side_effects=True, vmem_limit_bytes=56 * 1024 * 1024
        ),
    )(
        hidden,
        self_norm[None],
        cross_norm[None],
        cosine,
        sine,
        query_gain[None],
        key_gain[None],
        cache_lengths,
        cross_gate,
        tile_count,
        tile_place,
        self_query,
        self_keyval,
        self_output,
        key_cache,
        cross_query,
        cross_output,
        image_keyval,
    )
    return result.astype(BF16)


def solution(mesh):
    in_specs = (
        P(("groups", "batch"), None),
        P(),
        P("batch", "tensor"),
        P("batch", "tensor"),
        P("tensor", "batch"),
        P(("groups", "batch"), None, "tensor"),
        P(("groups", "batch")),
        P(),
        P("batch", "tensor"),
        P(),
        P(),
        P("tensor", "batch"),
        P(),
        P(("groups", "batch"), None, "tensor"),
        P("groups"),
        P("groups", None),
    )
    out_specs = P(("groups", "batch"), None)
    return jax.shard_map(
        per_device, mesh=mesh, in_specs=in_specs, out_specs=out_specs, check_vma=False
    )
```

```python
import functools

import jax
import jax.numpy as jnp
from jax import lax
from jax.experimental import pallas as pl
from jax.experimental.pallas import tpu as pltpu
from jax.sharding import PartitionSpec as P

HEAD_DIM = 128
MAX_TILES = 4
EPSILON = 1e-05
THETA = 500000.0
CHUNKS = 4
COLS = 256
LOW = -1e30

F32 = jnp.float32
BF16 = jnp.bfloat16


def kernel(
    dims,
    hidden,
    self_norm,
    cross_norm,
    cosine,
    sine,
    query_gain,
    key_gain,
    lengths,
    gate,
    counts,
    places,
    self_query,
    self_keyval,
    self_output,
    key_cache,
    cross_query,
    cross_output,
    image_keyval,
    out,
    w_sq,
    w_kv,
    w_so,
    w_cq,
    w_co,
    cache,
    image,
    keys,
    h_send,
    h_recv,
    p_send,
    p_recv,
    a_send,
    a_recv,
    parts,
    stage,
    s_send,
    s_recv,
    c_stage,
    c_send,
    c_recv,
    o_send,
    o_recv,
    x_send,
    x_recv,
    f_send,
    f_recv,
    lhs,
    factor_rep,
    norm_rows,
    trig,
    a_rows,
    load_sem,
    send_sem,
    recv_sem,
):
    batch, tensor, width, kv_width, model, tokens = dims
    requests = batch
    depth = model // batch
    heads = width // HEAD_DIM
    kv_heads = kv_width // (2 * HEAD_DIM)
    group = heads // kv_heads
    slots = image_keyval.shape[0]
    scale = HEAD_DIM ** (-0.5)
    me = lax.axis_index("batch")
    mine = lax.axis_index("tensor")

    loads = {}

    def load(name, source, target, at, pieces=CHUNKS):
        rows = source.shape[0] // pieces
        loads[name] = [
            pltpu.make_async_copy(
                source.at[pl.ds(i * rows, rows)],
                target.at[pl.ds(i * rows, rows)],
                load_sem.at[at + i],
            )
            for i in range(pieces)
        ]

    load("sq", self_query, w_sq, 0)
    load("kv", self_keyval, w_kv, CHUNKS)
    load("so", self_output, w_so, 2 * CHUNKS)
    load("cq", cross_query, w_cq, 3 * CHUNKS)
    load("co", cross_output, w_co, 4 * CHUNKS)
    load("cache", key_cache.at[0], cache, 5 * CHUNKS)
    loads["image"] = [
        pltpu.make_async_copy(
            image_keyval.at[s], image.at[pl.ds(s * tokens, tokens)], load_sem.at[6 * CHUNKS + s]
        )
        for s in range(slots)
    ]

    def start(*names):
        for name in names:
            for copy in loads[name]:
                copy.start()

    def arrive(*names):
        for name in names:
            for copy in loads[name]:
                copy.wait()

    start("sq", "kv", "cache")

    barrier = pltpu.get_barrier_semaphore()
    for d in range(1, batch):
        pl.semaphore_signal(
            barrier,
            inc=1,
            device_id={"batch": lax.rem(me + d, batch)},
            device_id_type=pl.DeviceIdType.MESH,
        )
    for d in range(1, tensor):
        pl.semaphore_signal(
            barrier,
            inc=1,
            device_id={"tensor": lax.rem(mine + d, tensor)},
            device_id_type=pl.DeviceIdType.MESH,
        )
    for j in range(batch):
        columns = slice(j * depth, (j + 1) * depth)
        h_send[j] = hidden[:, columns].astype(F32)
        norm_rows[0, j] = self_norm[columns].astype(F32).reshape(1, depth)
        norm_rows[1, j] = cross_norm[columns].astype(F32).reshape(1, depth)
    h_recv[me] = h_send[me]
    half = HEAD_DIM // 2
    trig[0:1, 0:half] = cosine[...]
    trig[0:1, half:HEAD_DIM] = cosine[...]
    trig[1:2, 0:half] = -sine[...]
    trig[1:2, half:HEAD_DIM] = sine[...]
    pl.semaphore_wait(barrier, batch + tensor - 2)

    pending = []

    def exchange(phase, axis, count, index, source, target):
        copies = []
        for d in range(1, count):
            to = lax.rem(index + d, count)
            copy = pltpu.make_async_remote_copy(
                src_ref=source(to),
                dst_ref=target.at[index],
                send_sem=send_sem.at[phase, d],
                recv_sem=recv_sem.at[phase, d],
                device_id={axis: to},
                device_id_type=pl.DeviceIdType.MESH,
            )
            copy.start()
            copies.append(copy)
        pending.extend(copies)
        return copies

    def received(copies):
        for copy in copies:
            copy.wait_recv()

    def total(ref, count):
        value = ref[0].astype(F32)
        for j in range(1, count):
            value = value + ref[j].astype(F32)
        return value

    def thirds(value):
        high = value.astype(BF16).astype(F32)
        middle = (value - high).astype(BF16).astype(F32)
        return high, middle, value - high - middle

    def multiply(left, weight, columns, store):
        @pl.loop(0, columns // COLS)
        def _(i):
            part = jnp.dot(
                left, weight[:, pl.ds(pl.multiple_of(i * COLS, COLS), COLS)],
                preferred_element_type=F32,
            )
            store(i, part)

    per_tile = COLS // HEAD_DIM

    copies = exchange(0, "batch", batch, me, lambda to: h_send.at[to], h_recv)
    received(copies)
    for r in range(requests):
        lhs[pl.ds(r, 1), 0:depth] = h_recv[r]
    hidden_cols = lhs[:, 0:depth]
    squares = jnp.sum(hidden_cols * hidden_cols, axis=1, keepdims=True)
    left = (hidden_cols * norm_rows[0, me]).astype(BF16)

    qkv_rows = heads + 2 * kv_heads

    def store_rows(base):
        def store(i, part):
            for r in range(requests):
                for c in range(per_tile):
                    p_send[r, pl.ds(base + i * per_tile + c, 1), :] = part[
                        r : r + 1, c * HEAD_DIM : (c + 1) * HEAD_DIM
                    ]

        return store

    for r in range(requests):
        p_send[r, pl.ds(qkv_rows, 1), :] = jnp.broadcast_to(squares[r : r + 1], (1, HEAD_DIM))
    arrive("sq", "kv")
    start("so", "image", "cq", "co")
    multiply(left, w_sq, width, store_rows(0))
    multiply(left, w_kv, kv_width, store_rows(heads))
    p_recv[me] = p_send[me]
    copies = exchange(1, "batch", batch, me, lambda to: p_send.at[to], p_recv)
    arrive("cache")
    received(copies)
    projected = total(p_recv, batch)
    factor = lax.rsqrt(projected[qkv_rows : qkv_rows + 1] * (1.0 / model) + EPSILON)
    projected = projected * factor
    rotated = projected * trig[0:1, :] + pltpu.roll(projected, HEAD_DIM // 2, 1) * trig[1:2, :]

    position = lax.broadcasted_iota(jnp.int32, (group, cache.shape[0]), 1)
    usable = position < lengths[0]
    for k in range(kv_heads):
        query = rotated[k * group : (k + 1) * group].astype(BF16)
        at = heads + 2 * k
        fresh_key = rotated[at : at + 1].astype(BF16).astype(F32)
        fresh_value = projected[at + 1 : at + 2].astype(BF16).astype(F32)
        base = 2 * k * HEAD_DIM
        scores = (
            lax.dot_general(
                query,
                cache[:, base : base + HEAD_DIM],
                (((1,), (1,)), ((), ())),
                preferred_element_type=F32,
            )
            * scale
        )
        scores = jnp.where(usable, scores, LOW)
        own_score = jnp.sum(query.astype(F32) * fresh_key, axis=1, keepdims=True) * scale
        top = jnp.maximum(jnp.max(scores, axis=1, keepdims=True), own_score)
        weights = jnp.exp(scores - top)
        own_weight = jnp.exp(own_score - top)
        inverse = 1.0 / (jnp.sum(weights, axis=1, keepdims=True) + own_weight)
        mixed = jnp.dot(
            (weights * inverse).astype(BF16),
            cache[:, base + HEAD_DIM : base + 2 * HEAD_DIM],
            preferred_element_type=F32,
        )
        own_prob = (own_weight * inverse).astype(BF16).astype(F32)
        a_rows[0, k * group : (k + 1) * group, :] = mixed + own_prob * fresh_value
    a_send[...] = a_rows[0].astype(BF16)
    a_recv[me] = a_send[...]
    copies = exchange(2, "batch", batch, me, lambda to: a_send, a_recv)
    first = me * slots
    owners = [jnp.int32(-1)] * slots
    for r in range(requests):
        for j in range(MAX_TILES):
            at = jnp.where(j < counts[r], places[r, j] - first, -1)
            owners = [jnp.where(at == s, r, owner) for s, owner in enumerate(owners)]
    arrive("so")
    received(copies)

    for r in range(requests):
        a_rows[r] = a_recv[r].astype(F32)
    for h in range(heads):
        lhs[:, h * HEAD_DIM : (h + 1) * HEAD_DIM] = a_rows[:, h, :]
    left = lhs[:, 0:width].astype(BF16)

    blocks = depth // HEAD_DIM

    def store_blocks(i, part):
        for c in range(per_tile):
            parts[i * per_tile + c] = part[:, c * HEAD_DIM : (c + 1) * HEAD_DIM]

    def pack(target):
        for c in range(blocks):
            stage[c * requests : (c + 1) * requests, :] = parts[c]
        target[...] = stage[...].astype(BF16)

    def unpack(ref):
        rows = total(ref, tensor)
        for c in range(blocks):
            lhs[:, c * HEAD_DIM : (c + 1) * HEAD_DIM] = rows[c * requests : (c + 1) * requests]
        return lhs[:, 0:depth]

    multiply(left, w_so, depth, store_blocks)
    pack(s_send)
    s_recv[mine] = s_send[...]
    copies = exchange(3, "tensor", tensor, mine, lambda to: s_send, s_recv)

    arrive("image")
    for k in range(kv_heads):
        base = 2 * k * HEAD_DIM
        for s in range(slots):
            rows = slice(s * tokens, (s + 1) * tokens)
            raw = image[rows, base : base + HEAD_DIM].astype(F32)
            inverse = lax.rsqrt(jnp.mean(raw * raw, axis=1, keepdims=True) + EPSILON)
            keys[k, rows, :] = (raw * inverse * key_gain[...]).astype(BF16)
    arrive("cq")
    received(copies)
    residual = (hidden_cols + unpack(s_recv)).astype(BF16).astype(F32)
    squares = jnp.sum(residual * residual, axis=1, keepdims=True)
    left = (residual * norm_rows[1, me]).astype(BF16)

    multiply(left, w_cq, width, store_blocks)
    for h in range(heads):
        c_stage[h * requests : (h + 1) * requests, :] = parts[h]
    lane = lax.broadcasted_iota(jnp.int32, (requests, HEAD_DIM), 1)
    split = jnp.zeros((requests, HEAD_DIM), F32)
    for i, third in enumerate(thirds(squares)):
        split = jnp.where(lane == i, third, split)
    rest = c_stage.shape[0] - heads * requests
    c_stage[heads * requests :, :] = jnp.zeros((rest, HEAD_DIM), F32)
    c_stage[heads * requests : (heads + 1) * requests, :] = split
    c_send[...] = c_stage[...].astype(BF16)
    c_recv[me] = c_send[...]
    copies = exchange(4, "batch", batch, me, lambda to: c_send, c_recv)
    received(copies)
    raw = total(c_recv, batch)
    squares = jnp.sum(raw[heads * requests : (heads + 1) * requests], axis=1, keepdims=True)
    factor = lax.rsqrt(squares * (1.0 / model) + EPSILON)
    factor = jnp.broadcast_to(factor, (requests, HEAD_DIM))
    for h in range(heads):
        factor_rep[h * requests : (h + 1) * requests, :] = factor
    raw = raw[0 : heads * requests] * factor_rep[...]
    inverse = lax.rsqrt(jnp.mean(raw * raw, axis=1, keepdims=True) + EPSILON)
    queries = (raw * inverse * query_gain[...]).astype(BF16)

    shape = (group * requests, slots * tokens)
    column = lax.broadcasted_iota(jnp.int32, shape, 1)
    owner = jnp.full(shape, owners[0])
    for s in range(1, slots):
        owner = jnp.where(column >= s * tokens, owners[s], owner)
    mask = lax.rem(lax.broadcasted_iota(jnp.int32, shape, 0), requests) == owner
    lane = lax.broadcasted_iota(jnp.int32, (group * requests, HEAD_DIM), 1)
    stats = jnp.zeros((group * requests, HEAD_DIM), F32)
    for k in range(kv_heads):
        base = (2 * k + 1) * HEAD_DIM
        rows = slice(k * group * requests, (k + 1) * group * requests)
        scores = (
            lax.dot_general(
                queries[rows], keys[k], (((1,), (1,)), ((), ())), preferred_element_type=F32
            )
            * scale
        )
        scores = jnp.where(mask, scores, LOW)
        top = jnp.max(scores, axis=1, keepdims=True)
        weights = jnp.where(mask, jnp.exp(scores - top), 0.0)
        amount = jnp.sum(weights, axis=1, keepdims=True)
        o_send[k] = jnp.dot(
            weights.astype(BF16), image[:, base : base + HEAD_DIM], preferred_element_type=F32
        ).astype(BF16)
        for i, third in enumerate(thirds(top) + thirds(amount)):
            stats = jnp.where(lane == 6 * k + i, third, stats)
    o_send[kv_heads] = stats.astype(BF16)
    o_recv[me] = o_send[...]
    copies = exchange(5, "batch", batch, me, lambda to: o_send, o_recv)
    arrive("co")
    received(copies)
    for k in range(kv_heads):
        at = 6 * k
        blocks_in = [o_recv[j, kv_heads].astype(F32) for j in range(batch)]
        tops, sums = [
            [
                b[:, i : i + 1] + b[:, i + 1 : i + 2] + b[:, i + 2 : i + 3]
                for b in blocks_in
            ]
            for i in (at, at + 3)
        ]
        peak = functools.reduce(jnp.maximum, tops)
        factors = [jnp.exp(top - peak) for top in tops]
        amount = sum(f * part for f, part in zip(factors, sums))
        crossed = sum(f * o_recv[j, k].astype(F32) for j, f in enumerate(factors)) / amount
        for g in range(group):
            h = k * group + g
            lhs[:, h * HEAD_DIM : (h + 1) * HEAD_DIM] = crossed[g * requests : (g + 1) * requests]
    left = lhs[:, 0:width].astype(BF16)

    multiply(left, w_co, depth, store_blocks)
    pack(x_send)
    x_recv[mine] = x_send[...]
    copies = exchange(6, "tensor", tensor, mine, lambda to: x_send, x_recv)
    gating = jnp.tanh(jnp.full((1, HEAD_DIM), gate[0]))[:, 0:1]
    received(copies)
    final = residual + gating * unpack(x_recv)
    for r in range(requests):
        f_send[r] = final[r : r + 1]
    f_recv[me] = f_send[me]
    copies = exchange(7, "batch", batch, me, lambda to: f_send.at[to], f_recv)
    received(copies)
    for j in range(batch):
        out[:, j * depth : (j + 1) * depth] = f_recv[j]
    for copy in pending:
        copy.wait_send()


def per_device(
    hidden,
    self_norm,
    self_query,
    self_keyval,
    self_output,
    key_cache,
    cache_lengths,
    cross_norm,
    cross_query,
    query_gain,
    key_gain,
    cross_output,
    cross_gate,
    image_keyval,
    tile_count,
    tile_place,
):
    batch = lax.axis_size("batch")
    tensor = lax.axis_size("tensor")
    assert hidden.shape[0] == 1
    model = hidden.shape[1]
    depth = model // batch
    width = self_query.shape[1]
    kv_width = self_keyval.shape[1]
    heads = width // HEAD_DIM
    kv_heads = kv_width // (2 * HEAD_DIM)
    group = heads // kv_heads
    slots, tokens = image_keyval.shape[:2]
    requests = batch

    half = HEAD_DIM // 2
    frequency = THETA ** (-(jnp.arange(half, dtype=F32) * 2.0 / HEAD_DIM))
    angles = cache_lengths.astype(F32)[:, None] * frequency[None, :]
    cosine, sine = jnp.cos(angles), jnp.sin(angles)
    vmem = pl.BlockSpec(memory_space=pltpu.VMEM)
    smem = pl.BlockSpec(memory_space=pltpu.SMEM)
    anywhere = pl.BlockSpec(memory_space=pl.ANY)
    qkv_rows = -(-(heads + 2 * kv_heads + 1) // 8) * 8
    cross_rows = -(-(heads + 1) * requests // 16) * 16
    head_rows = -(-heads // 16) * 16
    blocks = depth // HEAD_DIM
    sum_rows = blocks * requests
    dims = (batch, tensor, width, kv_width, model, tokens)
    result = pl.pallas_call(
        functools.partial(kernel, dims),
        out_shape=jax.ShapeDtypeStruct((1, model), F32),
        in_specs=[vmem] * 7 + [smem] * 4 + [anywhere] * 7,
        out_specs=vmem,
        scratch_shapes=[
            pltpu.VMEM(self_query.shape, BF16),
            pltpu.VMEM(self_keyval.shape, BF16),
            pltpu.VMEM(self_output.shape, BF16),
            pltpu.VMEM(cross_query.shape, BF16),
            pltpu.VMEM(cross_output.shape, BF16),
            pltpu.VMEM(key_cache.shape[1:], BF16),
            pltpu.VMEM((slots * tokens, kv_width), BF16),
            pltpu.VMEM((kv_heads, slots * tokens, HEAD_DIM), BF16),
            pltpu.VMEM((batch, 1, depth), F32),
            pltpu.VMEM((batch, 1, depth), F32),
            pltpu.VMEM((batch, qkv_rows, HEAD_DIM), F32),
            pltpu.VMEM((batch, qkv_rows, HEAD_DIM), F32),
            pltpu.VMEM((head_rows, HEAD_DIM), BF16),
            pltpu.VMEM((batch, head_rows, HEAD_DIM), BF16),
            pltpu.VMEM((max(heads, blocks), requests, HEAD_DIM), F32),
            pltpu.VMEM((sum_rows, HEAD_DIM), F32),
            pltpu.VMEM((sum_rows, HEAD_DIM), BF16),
            pltpu.VMEM((tensor, sum_rows, HEAD_DIM), BF16),
            pltpu.VMEM((cross_rows, HEAD_DIM), F32),
            pltpu.VMEM((cross_rows, HEAD_DIM), BF16),
            pltpu.VMEM((batch, cross_rows, HEAD_DIM), BF16),
            pltpu.VMEM((kv_heads + 1, group * requests, HEAD_DIM), BF16),
            pltpu.VMEM((batch, kv_heads + 1, group * requests, HEAD_DIM), BF16),
            pltpu.VMEM((sum_rows, HEAD_DIM), BF16),
            pltpu.VMEM((tensor, sum_rows, HEAD_DIM), BF16),
            pltpu.VMEM((batch, 1, depth), F32),
            pltpu.VMEM((batch, 1, depth), F32),
            pltpu.VMEM((requests, max(width, depth)), F32),
            pltpu.VMEM((heads * requests, HEAD_DIM), F32),
            pltpu.VMEM((2, batch, 1, depth), F32),
            pltpu.VMEM((8, HEAD_DIM), F32),
            pltpu.VMEM((batch, head_rows, HEAD_DIM), F32),
            pltpu.SemaphoreType.DMA((6 * CHUNKS + slots,)),
            pltpu.SemaphoreType.DMA((8, max(batch, tensor))),
            pltpu.SemaphoreType.DMA((8, max(batch, tensor))),
        ],
        compiler_params=pltpu.CompilerParams(
            collective_id=0, has_side_effects=True, vmem_limit_bytes=56 * 1024 * 1024
        ),
    )(
        hidden,
        self_norm,
        cross_norm,
        cosine,
        sine,
        query_gain[None],
        key_gain[None],
        cache_lengths,
        cross_gate,
        tile_count,
        tile_place,
        self_query,
        self_keyval,
        self_output,
        key_cache,
        cross_query,
        cross_output,
        image_keyval,
    )
    return result.astype(BF16)


def solution(mesh):
    in_specs = (
        P(("groups", "batch"), None),
        P(),
        P("batch", "tensor"),
        P("batch", "tensor"),
        P("tensor", "batch"),
        P(("groups", "batch"), None, "tensor"),
        P(("groups", "batch")),
        P(),
        P("batch", "tensor"),
        P(),
        P(),
        P("tensor", "batch"),
        P(),
        P(("groups", "batch"), None, "tensor"),
        P("groups"),
        P("groups", None),
    )
    out_specs = P(("groups", "batch"), None)
    return jax.shard_map(
        per_device, mesh=mesh, in_specs=in_specs, out_specs=out_specs, check_vma=False
    )
```
